32 devices in a mesh: grp: 4 (over x, core), orb: 8 (over z, y).
Axes of the slice: x: 2, y: 2, z: 4, core: 2. Of those that a mesh axis runs over, the one named last changes fastest.
Arguments:
- df_panels: bfloat16 [32, 1024, 512], P(('grp', 'orb')), may hold values from -1.0546875 to 1.0546875
- occ_energy: float32 [32], replicated, may hold values from -2 to -0.5
- virt_energy: float32 [512], replicated, may hold values from 0.2 to 4
- fock_off: float32 [512, 512], replicated, may hold values from -0.25 to 0.25
- i_plan: int32 [3, 4], replicated, may hold values from 0 to 7
- pair_owner: int32 [384, 1], P(('grp', 'orb')), may hold values from 0 to 3; in each aligned block of 12 rows (0 to 11, 12 to 23, ...) at most 4 rows name the same one
- pair_weight: float32 [384], P(('grp', 'orb')), may hold values from -4 to 4
Outputs:
- residual: float32 [32, 512, 512], P(('grp', 'orb'))
The draws below stay inside these ranges and needn't reach their ends.
Inputs may be any that keep to these rules, and one draw needn't show every extreme that they name: `pair_owner`: each orbital's 12 rows name no group more than 4 times; some orbital names one group exactly 4 times.
All inputs are finite; a program needn't handle non-finite values.
Results may differ from the reference program's by a relative error of at most 0.0029.
Values may be sent and summed in bfloat16 or wider, within the bound.
A program may use at most 128 MiB of HBM per device.

```python
import math
import jax
import jax.numpy as jnp
import numpy as np
from jax import lax

NAUX = 1024
NVIR = 512
STEPS = 3
CAP = 4
NO = 32
NT = 12
N_GRP = 4
N_ORB = 8


def set_ends(array, own_key, smallest, top_value):
    longest = array.shape.index(max(array.shape))
    spots = []
    for shift in (0, 1):
        where = [jax.random.randint(jax.random.fold_in(own_key, axis), (), 0, length) for axis, length in enumerate(array.shape)]
        where[longest] = (where[longest] + shift) % array.shape[longest]
        spots.append(tuple(where))
    return array.at[spots[0]].set(smallest).at[spots[1]].set(top_value)


def block_scale(stream_key, extent, pieces, least, largest):
    level = 1.0
    for axis_at, blocks in pieces:
        draws = jax.random.uniform(jax.random.fold_in(jax.random.fold_in(stream_key, 6), axis_at), (blocks,), jnp.float32, least / len(pieces), largest / len(pieces))
        level = level * jnp.repeat(jnp.exp(draws), extent[axis_at] // blocks).reshape((-1,) + (1,) * (len(extent) - 1 - axis_at))
    return level


def shared_out(own_key, own, number, rows, amount, top, limit, slope):
    sequence = jax.random.permutation(own_key, amount)
    crowded, common = shares(amount, rows * top, limit, slope, True), shares(amount, rows * top, limit, slope, False)
    places = jnp.arange(amount)

    def named(sizes, turn):
        used = int((sizes > 0).sum())
        fixed = max(1, used // 4)
        shifted = fixed + (places - fixed + turn * (used - fixed)) % max(1, amount - fixed)
        return jnp.zeros((amount,), jnp.int32).at[sequence[jnp.where(places < fixed, places, shifted)]].set(jnp.asarray(sizes, jnp.int32))

    sizes = jnp.where(number % 4 == 0, named(crowded, number // 4), named(common, number - number // 4 - 1))
    mixed = jax.random.permutation(jax.random.fold_in(own, 3), amount)
    source_of, receiver = mixed[0:amount // 2 * 2:2], mixed[1:amount // 2 * 2:2]
    room = jnp.minimum(sizes[source_of] - 1, limit - sizes[receiver]) // 2
    room = jnp.where((source_of == sequence[0]) | (receiver == sequence[0]) | (sizes[receiver] == 0), 0, jnp.maximum(room, 0))
    shifted = jax.random.randint(jax.random.fold_in(own, 4), (amount // 2,), 0, 1 << 20) % (room + 1)
    sizes = sizes.at[source_of].add(-shifted).at[receiver].add(shifted)
    items = jnp.searchsorted(jnp.cumsum(sizes), jnp.arange(rows * top), side="right").astype(jnp.int32)
    listing = items.reshape(top, rows).T
    listing = listing[jax.random.permutation(jax.random.fold_in(own, 1), rows)]
    turn = jax.random.randint(jax.random.fold_in(own, 2), (rows, 1), 0, top)
    return jnp.take_along_axis(listing, (jnp.arange(top)[None, :] + turn) % top, axis=1)


def shares(number_of, total, reach, skew, full):
    portions = [(1 << 20) // math.isqrt(standing ** skew) + 1 for standing in range(1, number_of + 1)]
    largest = reach if full else min(reach, max(-(-total // number_of), total * portions[0] // sum(portions)))
    least = 1 if total - largest >= number_of - 1 else 0
    counts, spare = [largest] + [least] * (number_of - 1), total - largest - least * (number_of - 1)
    while spare > 0:
        free = [i for i in range(1, number_of) if counts[i] < largest] or [i for i in range(1, number_of) if counts[i] < reach]
        mass, left = sum([portions[i] for i in free]), spare
        for i in free:
            more = min(reach - counts[i], max(1, left * portions[i] // mass), spare)
            counts[i] = counts[i] + more
            spare = spare - more
    return np.array(counts)


def centred(key, extent, deviation, most, split=(), kind=jnp.bfloat16):
    drawn = jax.random.normal(key, extent, jnp.float32) * deviation
    if len(split) > 0:
        drawn = block_scale(key, extent, split, -0.22, 0.18) * drawn
    return jnp.clip(drawn, min=-most, max=most).astype(kind)


def setup_inputs(seed: int = 0) -> dict:
    streams_of = jax.random.split(jax.random.key(seed), 8)
    df_panels = centred(streams_of[0], (NO, NAUX, NVIR), (NAUX ** -0.25), 1.0546875, ((0, 32),))
    occ_energy = jnp.clip(jax.random.uniform(streams_of[1], (NO,), jnp.float32, -2.0, -0.5), -2.0, -0.5)
    virt_energy = jnp.clip(jnp.exp(jax.random.uniform(streams_of[2], (NVIR,), jnp.float32, math.log(0.2), math.log(4.0))), 0.2, 4.0)
    fock_off = centred(streams_of[3], (NVIR, NVIR), NVIR ** -0.5, 0.25, (), jnp.float32)
    i_plan = set_ends(jax.random.randint(streams_of[4], (STEPS, N_GRP), 0, N_ORB), jax.random.fold_in(streams_of[4], 1), 0, N_ORB - 1).astype(jnp.int32)
    pair_owner_keys = jax.random.split(jax.random.fold_in(streams_of[5], 1), (NO * NT) // NT)
    pair_owner_turns = jax.random.permutation(jax.random.fold_in(streams_of[5], 3), (NO * NT) // NT)
    pair_owner = jax.vmap(lambda own, number: shared_out(jax.random.fold_in(streams_of[5], 2), own, number, NT, N_GRP, 1, CAP, 2))(pair_owner_keys, pair_owner_turns).reshape((NO * NT, 1))
    pair_weight = centred(streams_of[6], (NO * NT,), 1.0, 4.0, ((0, 32),), jnp.float32)
    return dict(df_panels=df_panels, occ_energy=occ_energy, virt_energy=virt_energy, fock_off=fock_off, i_plan=i_plan, pair_owner=pair_owner, pair_weight=pair_weight)


def reference(df_panels, occ_energy, virt_energy, fock_off, i_plan, pair_owner, pair_weight):
    highest = lax.Precision.HIGHEST
    panels_wide = df_panels.astype(jnp.float32)
    fock_matrix = jnp.diag(virt_energy) + 0.5 * (fock_off + fock_off.T)
    pair_sum = virt_energy[:, None] + virt_energy[None, :]
    groups_range = jnp.arange(N_GRP, dtype=jnp.int32)
    owners = pair_owner[:, 0].reshape(NO, NT)
    weights = pair_weight.reshape(NO, NT)

    def per_device(summed, device):
        own_panel = panels_wide[device]
        own_energy = occ_energy[device]
        tiles = []
        for step_index in range(STEPS):
            i_ids = (groups_range * N_ORB + i_plan[step_index]).astype(jnp.int32)
            integral = jnp.einsum("gxa,xb->gab", panels_wide[i_ids], own_panel, precision=highest)
            denominator = pair_sum[None] - occ_energy[i_ids][:, None, None] - own_energy
            tiles.append(integral / denominator)
        scaled = (jnp.concatenate(tiles, 0) * weights[device][:, None, None]).astype(jnp.bfloat16).astype(jnp.float32)
        one_hot = (owners[device][:, None] == groups_range[None, :]).astype(jnp.float32)
        partial_value = jnp.einsum("tg,tab->gab", one_hot, scaled, precision=highest)
        targets = (groups_range * N_ORB + device % N_ORB).astype(jnp.int32)
        return summed.at[targets].add(partial_value), None

    start = jnp.zeros((NO, NVIR, NVIR), jnp.float32)
    summed = lax.scan(per_device, start, jnp.arange(NO, dtype=jnp.int32))[0]
    left = jnp.einsum("ab,dbc->dac", fock_matrix, summed, precision=highest)
    right = jnp.einsum("dab,bc->dac", summed, fock_matrix, precision=highest)
    return left + right
```

```python
import functools

import jax
import jax.numpy as jnp
from jax import lax
from jax.experimental import pallas as pl
from jax.experimental.pallas import tpu as pltpu
from jax.sharding import PartitionSpec as P

MESH = pl.DeviceIdType.MESH
ROWS = 8


def ring_orb(pos, n):
    half = n // 2
    return jnp.where(pos < half, 2 * pos, 2 * (n - 1 - pos) + 1)


def gather_kernel(
    ng, no, nt, ids, panel_t, panel, meta, gt, cols, metas,
    pieces, sel, sc_send, sc_recv, col_send, col_recv, meta_send, meta_recv,
    ring_send, ring_recv, loc,
):
    nall = ng * no
    g = lax.axis_index("grp")
    o = lax.axis_index("orb")
    me = g * no + o
    nvir, naux = panel_t.shape
    qa = nvir // ng
    ra = qa // ROWS
    nc = no // ROWS
    wa = naux // nc
    half_t = nt // 2

    def piece_of(orb):
        return orb // nc, orb % nc

    def block_in_panel(q, orb):
        r, c = piece_of(orb)
        return panel_t.at[
            pl.ds(pl.multiple_of(q * qa + r * ra, 16), ra), pl.ds(pl.multiple_of(c * wa, 128), wa)
        ]

    def scatter(k):
        to = lax.rem(me + k, nall)
        q, orb = to // no, lax.rem(to, no)
        return pltpu.make_async_remote_copy(
            src_ref=block_in_panel(q, orb),
            dst_ref=pieces.at[me],
            send_sem=sc_send.at[k],
            recv_sem=sc_recv.at[k],
            device_id=(q, orb),
            device_id_type=MESH,
        )

    own_piece = pltpu.make_async_copy(block_in_panel(g, o), pieces.at[me], loc.at[0])
    own_piece.start()

    def start_scatter(k, carry):
        scatter(k).start()
        return carry

    lax.fori_loop(1, nall, start_scatter, 0)

    gx, gc = g // 2, lax.rem(g, 2)
    core_peer = gx * 2 + 1 - gc
    x_peer = (1 - gx) * 2 + gc
    diag_peer = (1 - gx) * 2 + 1 - gc

    def column(index, src, slot, to):
        return pltpu.make_async_remote_copy(
            src_ref=src,
            dst_ref=cols.at[slot],
            send_sem=col_send.at[index],
            recv_sem=col_recv.at[index],
            device_id=(to, o),
            device_id_type=MESH,
        )

    across = column(0, panel, g, x_peer)
    beside = column(1, panel, g, core_peer)
    across.start()
    beside.start()
    own_col = pltpu.make_async_copy(panel, cols.at[g], loc.at[1])
    own_col.start()
    own_meta = pltpu.make_async_copy(meta, metas.at[g], loc.at[2])
    own_meta.start()
    meta_copies = []
    for index, to in enumerate((core_peer, x_peer, diag_peer)):
        copy = pltpu.make_async_remote_copy(
            src_ref=meta,
            dst_ref=metas.at[g],
            send_sem=meta_send.at[index],
            recv_sem=meta_recv.at[index],
            device_id=(to, o),
            device_id_type=MESH,
        )
        copy.start()
        meta_copies.append(copy)

    own_piece.wait()

    def wait_scatter(k, carry):
        scatter(k).wait_recv()
        return carry

    lax.fori_loop(1, nall, wait_scatter, 0)
    for t in range(nt):
        sel[t] = pieces[ids[t]]

    def block_in_gt(hf, orb):
        r, c = piece_of(orb)
        return gt.at[
            pl.ds(hf * half_t, half_t),
            pl.ds(pl.multiple_of(r * ra, 16), ra),
            pl.ds(pl.multiple_of(c * wa, 128), wa),
        ]

    r_me, c_me = piece_of(o)
    own_sel = pltpu.make_async_copy(
        sel,
        gt.at[
            :, pl.ds(pl.multiple_of(r_me * ra, 16), ra), pl.ds(pl.multiple_of(c_me * wa, 128), wa)
        ],
        loc.at[3],
    )
    own_sel.start()

    pos = jnp.where(lax.rem(o, 2) == 0, o // 2, no - 1 - o // 2)
    steps = no // 2
    next_orb = (
        ring_orb(lax.rem(pos + 1, no), no),
        ring_orb(lax.rem(pos + no - 1, no), no),
    )

    def ring(way, step, hf):
        origin = lax.rem(pos + (no - step if way == 0 else step), no)
        orb = ring_orb(origin, no)
        src = block_in_gt(hf, orb)
        if step == 0:
            src = sel.at[pl.ds(hf * half_t, half_t)]
        return pltpu.make_async_remote_copy(
            src_ref=src,
            dst_ref=block_in_gt(hf, orb),
            send_sem=ring_send.at[way, step, hf],
            recv_sem=ring_recv.at[way, step, hf],
            device_id=(g, next_orb[way]),
            device_id_type=MESH,
        )

    def used(way, step, hf):
        return step < steps - 1 or hf == way

    for step in range(steps):
        for hf in range(2):
            for way in range(2):
                if used(way, step, hf):
                    if step > 0:
                        ring(way, step - 1, hf).wait_recv()
                    ring(way, step, hf).start()
        if step == 0:
            across.wait_recv()
            onward = column(2, cols.at[x_peer], x_peer, core_peer)
            onward.start()

    for way in range(2):
        for step in range(steps):
            for hf in range(2):
                if used(way, step, hf):
                    if step == steps - 1 or not used(way, step + 1, hf):
                        ring(way, step, hf).wait_recv()
    beside.wait_recv()
    onward.wait_recv()
    for copy in meta_copies:
        copy.wait_recv()

    def wait_sent(k, carry):
        scatter(k).wait_send()
        return carry

    lax.fori_loop(1, nall, wait_sent, 0)
    across.wait_send()
    beside.wait_send()
    onward.wait_send()
    for copy in meta_copies:
        copy.wait_send()
    for way in range(2):
        for step in range(steps):
            for hf in range(2):
                if used(way, step, hf):
                    ring(way, step, hf).wait_send()
    own_col.wait()
    own_meta.wait()
    own_sel.wait()


def tiles_kernel(nt, metas, occ_i, gt, col, va, vb, out, acc):
    j = pl.program_id(0)
    ng = out.shape[0]
    qa = gt.shape[1]
    group = 4

    @pl.when(j == 0)
    def _():
        acc[...] = jnp.zeros_like(acc)

    base = va[...] + vb[...]
    own = metas[j, 0, 2 * nt]
    right = col[0]
    for first in range(0, nt, group):
        left = gt[first : first + group].reshape(group * qa, gt.shape[2])
        integral = jnp.dot(left, right, preferred_element_type=jnp.float32)
        for k in range(group):
            t = first + k
            weight = metas[j, 0, t]
            owner = metas[j, 0, nt + t].astype(jnp.int32)
            denominator = base - occ_i[t] - own
            amplitude = integral[k * qa : (k + 1) * qa] / denominator * weight
            acc[owner] = acc[owner] + amplitude.astype(jnp.bfloat16).astype(jnp.float32)

    @pl.when(j == ng - 1)
    def _():
        out[...] = acc[...].astype(out.dtype)


def fock_kernel(summed, high, low, out):
    s = summed[...]
    h = high[...]
    l = low[...]
    dot = functools.partial(jnp.dot, preferred_element_type=jnp.float32)
    out[...] = (dot(h, s) + dot(s, h)) + (dot(l, s) + dot(s, l))


def shards(df_panels, occ_energy, virt_energy, fock_off, i_plan, pair_owner, pair_weight):
    ng = lax.axis_size("grp")
    no = lax.axis_size("orb")
    g = lax.axis_index("grp")
    me = g * no + lax.axis_index("orb")
    panel = df_panels[0]
    naux, nvir = panel.shape
    nt = pair_owner.shape[0]
    qa = nvir // ng
    f32 = jnp.float32
    vmem = pl.BlockSpec(memory_space=pltpu.VMEM)
    smem = pl.BlockSpec(memory_space=pltpu.SMEM)
    hbm = pl.BlockSpec(memory_space=pl.ANY)
    dma = pltpu.SemaphoreType.DMA

    ids = (jnp.arange(ng, dtype=jnp.int32)[None, :] * no + i_plan).reshape(nt)
    own_energy = lax.dynamic_slice_in_dim(occ_energy, me, 1)
    row = jnp.concatenate([pair_weight, pair_owner[:, 0].astype(f32), own_energy])
    meta = jnp.zeros((8, 128), f32).at[0, : 2 * nt + 1].set(row)
    nc = no // ROWS
    gt, cols, metas = pl.pallas_call(
        functools.partial(gather_kernel, ng, no, nt),
        out_shape=[
            jax.ShapeDtypeStruct((nt, qa, naux), jnp.bfloat16),
            jax.ShapeDtypeStruct((ng, naux, nvir), jnp.bfloat16),
            jax.ShapeDtypeStruct((ng, 8, 128), f32),
        ],
        in_specs=[smem, hbm, hbm, hbm],
        out_specs=[hbm, hbm, hbm],
        scratch_shapes=[
            pltpu.VMEM((ng * no, qa // ROWS, naux // nc), jnp.bfloat16),
            pltpu.VMEM((nt, qa // ROWS, naux // nc), jnp.bfloat16),
            dma((ng * no,)),
            dma((ng * no,)),
            dma((3,)),
            dma((3,)),
            dma((3,)),
            dma((3,)),
            dma((2, no // 2, 2)),
            dma((2, no // 2, 2)),
            dma((4,)),
        ],
        compiler_params=pltpu.CompilerParams(has_side_effects=True),
        name="gather_panels",
    )(ids, panel.T, panel, meta)

    va = lax.dynamic_slice_in_dim(virt_energy, g * qa, qa)[:, None]
    parts = pl.pallas_call(
        functools.partial(tiles_kernel, nt),
        grid=(ng,),
        out_shape=jax.ShapeDtypeStruct((ng, qa, nvir), jnp.bfloat16),
        in_specs=[
            smem,
            smem,
            vmem,
            pl.BlockSpec((1, naux, nvir), lambda j: (j, 0, 0)),
            vmem,
            vmem,
        ],
        out_specs=vmem,
        scratch_shapes=[pltpu.VMEM((ng, qa, nvir), f32)],
        compiler_params=pltpu.CompilerParams(vmem_limit_bytes=48 * 2**20),
        name="pair_tiles",
    )(metas[:, :1, :], occ_energy[ids], gt, cols, va, virt_energy[None, :])

    summed = lax.all_to_all(parts, "grp", split_axis=0, concat_axis=0, tiled=True)
    summed = summed.reshape(nvir, nvir)
    fock = jnp.diag(virt_energy) + 0.5 * (fock_off + fock_off.T)
    high = fock.astype(jnp.bfloat16)
    low = (fock - high.astype(f32)).astype(jnp.bfloat16)
    residual = pl.pallas_call(
        fock_kernel,
        out_shape=jax.ShapeDtypeStruct((nvir, nvir), f32),
        in_specs=[vmem] * 3,
        out_specs=vmem,
        compiler_params=pltpu.CompilerParams(vmem_limit_bytes=48 * 2**20),
        name="fock_products",
    )(summed, high, low)
    return residual[None]


def solution(mesh):
    placed = (
        P(("grp", "orb"), None, None),
        P(),
        P(),
        P(),
        P(),
        P(("grp", "orb"), None),
        P(("grp", "orb")),
    )
    return jax.shard_map(
        shards, mesh=mesh, in_specs=placed, out_specs=P(("grp", "orb"), None, None), check_vma=False
    )
```

```python
import functools

import jax
import jax.numpy as jnp
from jax import lax
from jax.experimental import pallas as pl
from jax.experimental.pallas import tpu as pltpu
from jax.sharding import PartitionSpec as P

MESH = pl.DeviceIdType.MESH
ROWS = 8


def ring_orb(pos, n):
    half = n // 2
    return jnp.where(pos < half, 2 * pos, 2 * (n - 1 - pos) + 1)


def gather_kernel(
    ng, no, nt, plan, weight, owner, panel_t, panel, gt, cols, metas,
    meta, pieces_here, pieces_over, sel, sc_send, sc_recv, col_send, col_recv, meta_send, meta_recv,
    ring_send, ring_recv, loc,
):
    g = lax.axis_index("grp")
    o = lax.axis_index("orb")
    nvir, naux = panel_t.shape
    qa = nvir // ng
    ra = qa // ROWS
    nc = no // ROWS
    wa = naux // nc
    half_t = nt // 2

    def piece_of(orb):
        return orb // nc, orb % nc

    def block_in_panel(q, orb):
        r, c = piece_of(orb)
        return panel_t.at[
            pl.ds(pl.multiple_of(q * qa + r * ra, 16), ra), pl.ds(pl.multiple_of(c * wa, 128), wa)
        ]

    pieces = (pieces_here, pieces_over)
    gx, gc = g // 2, lax.rem(g, 2)
    side = 2 * no
    place = gc * no + o

    def scatter(hf, k):
        to = lax.rem(gx + hf, 2) * side + lax.rem(place + k, side)
        q, orb = to // no, lax.rem(to, no)
        return pltpu.make_async_remote_copy(
            src_ref=block_in_panel(q, orb),
            dst_ref=pieces[hf].at[place],
            send_sem=sc_send.at[hf, k],
            recv_sem=sc_recv.at[hf, k],
            device_id=(q, orb),
            device_id_type=MESH,
        )

    own_piece = pltpu.make_async_copy(block_in_panel(g, o), pieces_here.at[place], loc.at[0])
    own_piece.start()

    def each_scatter(hf, act):
        def body(k, carry):
            act(scatter(hf, k))
            return carry

        lax.fori_loop(1 - hf, side, body, 0)

    each_scatter(0, lambda copy: copy.start())
    each_scatter(1, lambda copy: copy.start())
    meta[...] = jnp.zeros_like(meta)
    meta[0:1, 0:nt] = weight[...]
    meta[1:2, 0:nt] = owner[...].astype(jnp.float32)

    core_peer = gx * 2 + 1 - gc
    x_peer = (1 - gx) * 2 + gc
    diag_peer = (1 - gx) * 2 + 1 - gc

    def column(index, src, slot, to):
        return pltpu.make_async_remote_copy(
            src_ref=src,
            dst_ref=cols.at[slot],
            send_sem=col_send.at[index],
            recv_sem=col_recv.at[index],
            device_id=(to, o),
            device_id_type=MESH,
        )

    across = column(0, panel, g, x_peer)
    beside = column(1, panel, g, core_peer)
    across.start()
    beside.start()
    own_col = pltpu.make_async_copy(panel, cols.at[g], loc.at[1])
    own_col.start()
    own_meta = pltpu.make_async_copy(meta, metas.at[g], loc.at[2])
    own_meta.start()
    meta_copies = []
    for index, to in enumerate((core_peer, x_peer, diag_peer)):
        copy = pltpu.make_async_remote_copy(
            src_ref=meta,
            dst_ref=metas.at[g],
            send_sem=meta_send.at[index],
            recv_sem=meta_recv.at[index],
            device_id=(to, o),
            device_id_type=MESH,
        )
        copy.start()
        meta_copies.append(copy)

    own_piece.wait()

    def select(hf):
        side_x = lax.rem(gx + hf, 2)
        for c in range(2):
            for s in range(nt // ng):
                h = side_x * 2 + c
                sel[hf * half_t + c * (nt // ng) + s] = pieces[hf][c * no + plan[s, h]]

    def block_in_gt(hf, orb):
        r, c = piece_of(orb)
        return gt.at[
            pl.ds(hf * half_t, half_t),
            pl.ds(pl.multiple_of(r * ra, 16), ra),
            pl.ds(pl.multiple_of(c * wa, 128), wa),
        ]

    own_sel = [
        pltpu.make_async_copy(
            sel.at[pl.ds(hf * half_t, half_t)], block_in_gt(hf, o), loc.at[3 + hf]
        )
        for hf in range(2)
    ]

    pos = jnp.where(lax.rem(o, 2) == 0, o // 2, no - 1 - o // 2)
    steps = no // 2
    next_orb = (
        ring_orb(lax.rem(pos + 1, no), no),
        ring_orb(lax.rem(pos + no - 1, no), no),
    )

    def ring(way, step, hf):
        origin = lax.rem(pos + (no - step if way == 0 else step), no)
        orb = ring_orb(origin, no)
        src = block_in_gt(hf, orb)
        if step == 0:
            src = sel.at[pl.ds(hf * half_t, half_t)]
        return pltpu.make_async_remote_copy(
            src_ref=src,
            dst_ref=block_in_gt(hf, orb),
            send_sem=ring_send.at[way, step, hf],
            recv_sem=ring_recv.at[way, step, hf],
            device_id=(g, next_orb[way]),
            device_id_type=MESH,
        )

    def used(way, step, hf):
        return step < steps - 1 or hf == way

    for step in range(steps):
        for hf in range(2):
            if step == 0:
                each_scatter(hf, lambda copy: copy.wait_recv())
                select(hf)
                own_sel[hf].start()
            for way in range(2):
                if used(way, step, hf):
                    if step > 0:
                        ring(way, step - 1, hf).wait_recv()
                    ring(way, step, hf).start()
        if step == 0:
            across.wait_recv()
            onward = column(2, cols.at[x_peer], x_peer, core_peer)
            onward.start()

    for way in range(2):
        for step in range(steps):
            for hf in range(2):
                if used(way, step, hf):
                    if step == steps - 1 or not used(way, step + 1, hf):
                        ring(way, step, hf).wait_recv()
    beside.wait_recv()
    onward.wait_recv()
    for copy in meta_copies:
        copy.wait_recv()

    each_scatter(0, lambda copy: copy.wait_send())
    each_scatter(1, lambda copy: copy.wait_send())
    across.wait_send()
    beside.wait_send()
    onward.wait_send()
    for copy in meta_copies:
        copy.wait_send()
    for way in range(2):
        for step in range(steps):
            for hf in range(2):
                if used(way, step, hf):
                    ring(way, step, hf).wait_send()
    own_col.wait()
    own_meta.wait()
    for copy in own_sel:
        copy.wait()


def tiles_kernel(nt, group, no, metas, plan, occ, gt, cols, virt, out, acc, base):
    part = pl.program_id(0)
    j = pl.program_id(1)
    ng = out.shape[0]
    qa = gt.shape[1]
    steps = nt // ng
    g = lax.axis_index("grp")
    o = lax.axis_index("orb")

    @pl.when((j == 0) & (part == 0))
    def _():
        acc[...] = jnp.zeros_like(acc)
        rows = jnp.broadcast_to(virt[:, pl.ds(pl.multiple_of(g * qa, 128), qa)], (qa, qa)).T
        for k in range(out.shape[2] // qa):
            at = slice(k * qa, (k + 1) * qa)
            base[:, at] = rows + virt[:, at]

    own = occ[j * no + o]
    left = gt[...].reshape(group * qa, gt.shape[2])
    integral = jnp.dot(left, cols[0], preferred_element_type=jnp.float32)
    for k in range(group):
        slot = part * group + k
        hf, rest = slot // (nt // 2), lax.rem(slot, nt // 2)
        c, s = rest // steps, lax.rem(rest, steps)
        h = lax.rem(g // 2 + hf, 2) * 2 + c
        t = s * ng + h
        weight = metas[j, 0, t]
        owner = metas[j, 1, t].astype(jnp.int32)
        denominator = base[...] - occ[h * no + plan[s, h]] - own
        amplitude = integral[k * qa : (k + 1) * qa] / denominator * weight
        acc[owner] = acc[owner] + amplitude.astype(jnp.bfloat16).astype(jnp.float32)

    @pl.when((j == ng - 1) & (part == pl.num_programs(0) - 1))
    def _():
        out[...] = acc[...].astype(out.dtype)


def split_kernel(virt, off, high, low):
    n = off.shape[0]
    rows = lax.broadcasted_iota(jnp.int32, (n, n), 0)
    columns = lax.broadcasted_iota(jnp.int32, (n, n), 1)
    fock = jnp.where(rows == columns, virt[...], 0.0) + 0.5 * (off[...] + off[...].T)
    top = fock.astype(jnp.bfloat16)
    high[...] = top
    low[...] = (fock - top.astype(jnp.float32)).astype(jnp.bfloat16)


def fock_kernel(summed, high, low, out):
    s = summed[...]
    h = high[...]
    l = low[...]
    dot = functools.partial(jnp.dot, preferred_element_type=jnp.float32)
    out[...] = (dot(h, s) + dot(s, h)) + (dot(l, s) + dot(s, l))


def shards(df_panels, occ_energy, virt_energy, fock_off, i_plan, pair_owner, pair_weight):
    ng = lax.axis_size("grp")
    no = lax.axis_size("orb")
    panel = df_panels[0]
    naux, nvir = panel.shape
    nt = pair_owner.shape[0]
    qa = nvir // ng
    f32 = jnp.float32
    vmem = pl.BlockSpec(memory_space=pltpu.VMEM)
    smem = pl.BlockSpec(memory_space=pltpu.SMEM)
    hbm = pl.BlockSpec(memory_space=pl.ANY)
    dma = pltpu.SemaphoreType.DMA

    nc = no // ROWS
    gt, cols, metas = pl.pallas_call(
        functools.partial(gather_kernel, ng, no, nt),
        out_shape=[
            jax.ShapeDtypeStruct((nt, qa, naux), jnp.bfloat16),
            jax.ShapeDtypeStruct((ng, naux, nvir), jnp.bfloat16),
            jax.ShapeDtypeStruct((ng, 8, 128), f32),
        ],
        in_specs=[smem, vmem, vmem, hbm, hbm],
        out_specs=[hbm, hbm, hbm],
        scratch_shapes=[
            pltpu.VMEM((8, 128), f32),
            pltpu.VMEM((2 * no, qa // ROWS, naux // nc), jnp.bfloat16),
            pltpu.VMEM((2 * no, qa // ROWS, naux // nc), jnp.bfloat16),
            pltpu.VMEM((nt, qa // ROWS, naux // nc), jnp.bfloat16),
            dma((2, 2 * no)),
            dma((2, 2 * no)),
            dma((3,)),
            dma((3,)),
            dma((3,)),
            dma((3,)),
            dma((2, no // 2, 2)),
            dma((2, no // 2, 2)),
            dma((5,)),
        ],
        compiler_params=pltpu.CompilerParams(has_side_effects=True),
        name="gather_panels",
    )(i_plan, pair_weight.reshape(1, nt), pair_owner.reshape(1, nt), panel.T, panel)

    virt_row = virt_energy[None, :]
    group = 4
    parts = pl.pallas_call(
        functools.partial(tiles_kernel, nt, group, no),
        grid=(nt // group, ng),
        out_shape=jax.ShapeDtypeStruct((ng, qa, nvir), jnp.bfloat16),
        in_specs=[
            smem,
            smem,
            smem,
            pl.BlockSpec((group, qa, naux), lambda p, j: (p, 0, 0)),
            pl.BlockSpec((1, naux, nvir), lambda p, j: (j, 0, 0)),
            vmem,
        ],
        out_specs=vmem,
        scratch_shapes=[pltpu.VMEM((ng, qa, nvir), f32), pltpu.VMEM((qa, nvir), f32)],
        compiler_params=pltpu.CompilerParams(vmem_limit_bytes=60 * 2**20),
        name="pair_tiles",
    )(metas, i_plan, occ_energy, gt, cols, virt_row)

    summed = lax.all_to_all(parts, "grp", split_axis=0, concat_axis=0, tiled=True)
    summed = summed.reshape(nvir, nvir)
    high, low = pl.pallas_call(
        split_kernel,
        out_shape=[jax.ShapeDtypeStruct((nvir, nvir), jnp.bfloat16)] * 2,
        in_specs=[vmem] * 2,
        out_specs=[vmem] * 2,
        cost_estimate=pl.CostEstimate(flops=4 * nvir * nvir, bytes_accessed=8 * nvir * nvir, transcendentals=0),
        name="fock_split",
    )(virt_row, fock_off)
    residual = pl.pallas_call(
        fock_kernel,
        out_shape=jax.ShapeDtypeStruct((nvir, nvir), f32),
        in_specs=[vmem] * 3,
        out_specs=vmem,
        compiler_params=pltpu.CompilerParams(vmem_limit_bytes=48 * 2**20),
        name="fock_products",
    )(summed, high, low)
    return residual[None]


def solution(mesh):
    placed = (
        P(("grp", "orb"), None, None),
        P(),
        P(),
        P(),
        P(),
        P(("grp", "orb"), None),
        P(("grp", "orb")),
    )
    return jax.shard_map(
        shards, mesh=mesh, in_specs=placed, out_specs=P(("grp", "orb"), None, None), check_vma=False
    )
```

```python
import functools

import jax
import jax.numpy as jnp
from jax import lax
from jax.experimental import pallas as pl
from jax.experimental.pallas import tpu as pltpu
from jax.sharding import PartitionSpec as P

MESH = pl.DeviceIdType.MESH
ROWS = 8


def ring_orb(pos, n):
    half = n // 2
    return jnp.where(pos < half, 2 * pos, 2 * (n - 1 - pos) + 1)


def gather_kernel(
    ng, no, nt, plan, weight, owner, panel_t, panel, gt, cols, metas,
    meta, pieces_here, pieces_over, sel, sc_send, sc_recv, col_send, col_recv, meta_send, meta_recv,
    ring_send, ring_recv, loc,
):
    g = lax.axis_index("grp")
    o = lax.axis_index("orb")
    nvir, naux = panel_t.shape
    qa = nvir // ng
    ra = qa // ROWS
    nc = no // ROWS
    wa = naux // nc
    half_t = nt // 2

    def piece_of(orb):
        return orb // nc, orb % nc

    def block_in_panel(q, orb):
        r, c = piece_of(orb)
        return panel_t.at[
            pl.ds(pl.multiple_of(q * qa + r * ra, 16), ra), pl.ds(pl.multiple_of(c * wa, 128), wa)
        ]

    pieces = (pieces_here, pieces_over)
    gx, gc = g // 2, lax.rem(g, 2)
    side = 2 * no
    place = gc * no + o

    def scatter(hf, k):
        to = lax.rem(gx + hf, 2) * side + lax.rem(place + k, side)
        q, orb = to // no, lax.rem(to, no)
        return pltpu.make_async_remote_copy(
            src_ref=block_in_panel(q, orb),
            dst_ref=pieces[hf].at[place],
            send_sem=sc_send.at[hf, k],
            recv_sem=sc_recv.at[hf, k],
            device_id=(q, orb),
            device_id_type=MESH,
        )

    own_piece = pltpu.make_async_copy(block_in_panel(g, o), pieces_here.at[place], loc.at[0])
    own_piece.start()

    def each_scatter(hf, act):
        def body(k, carry):
            act(scatter(hf, k))
            return carry

        lax.fori_loop(1 - hf, side, body, 0)

    each_scatter(0, lambda copy: copy.start())
    each_scatter(1, lambda copy: copy.start())
    meta[...] = jnp.zeros_like(meta)
    meta[0:1, 0:nt] = weight[...]
    meta[1:2, 0:nt] = owner[...].astype(jnp.float32)

    core_peer = gx * 2 + 1 - gc
    x_peer = (1 - gx) * 2 + gc
    diag_peer = (1 - gx) * 2 + 1 - gc

    def column(index, src, slot, to):
        return pltpu.make_async_remote_copy(
            src_ref=src,
            dst_ref=cols.at[slot],
            send_sem=col_send.at[index],
            recv_sem=col_recv.at[index],
            device_id=(to, o),
            device_id_type=MESH,
        )

    across = column(0, panel, g, x_peer)
    beside = column(1, panel, g, core_peer)
    across.start()
    beside.start()
    own_col = pltpu.make_async_copy(panel, cols.at[g], loc.at[1])
    own_col.start()
    own_meta = pltpu.make_async_copy(meta, metas.at[g], loc.at[2])
    own_meta.start()
    meta_copies = []
    for index, to in enumerate((core_peer, x_peer, diag_peer)):
        copy = pltpu.make_async_remote_copy(
            src_ref=meta,
            dst_ref=metas.at[g],
            send_sem=meta_send.at[index],
            recv_sem=meta_recv.at[index],
            device_id=(to, o),
            device_id_type=MESH,
        )
        copy.start()
        meta_copies.append(copy)

    own_piece.wait()

    def select(hf):
        side_x = lax.rem(gx + hf, 2)
        for c in range(2):
            for s in range(nt // ng):
                h = side_x * 2 + c
                sel[hf * half_t + c * (nt // ng) + s] = pieces[hf][c * no + plan[s, h]]

    def block_in_gt(hf, orb):
        r, c = piece_of(orb)
        return gt.at[
            pl.ds(hf * half_t, half_t),
            pl.ds(pl.multiple_of(r * ra, 16), ra),
            pl.ds(pl.multiple_of(c * wa, 128), wa),
        ]

    own_sel = [
        pltpu.make_async_copy(
            sel.at[pl.ds(hf * half_t, half_t)], block_in_gt(hf, o), loc.at[3 + hf]
        )
        for hf in range(2)
    ]

    pos = jnp.where(lax.rem(o, 2) == 0, o // 2, no - 1 - o // 2)
    steps = no // 2
    next_orb = (
        ring_orb(lax.rem(pos + 1, no), no),
        ring_orb(lax.rem(pos + no - 1, no), no),
    )

    def ring(way, step, hf):
        origin = lax.rem(pos + (no - step if way == 0 else step), no)
        orb = ring_orb(origin, no)
        src = block_in_gt(hf, orb)
        if step == 0:
            src = sel.at[pl.ds(hf * half_t, half_t)]
        return pltpu.make_async_remote_copy(
            src_ref=src,
            dst_ref=block_in_gt(hf, orb),
            send_sem=ring_send.at[way, step, hf],
            recv_sem=ring_recv.at[way, step, hf],
            device_id=(g, next_orb[way]),
            device_id_type=MESH,
        )

    def used(way, step, hf):
        return step < steps - 1 or hf == way

    for step in range(steps):
        for hf in range(2):
            if step == 0:
                each_scatter(hf, lambda copy: copy.wait_recv())
                select(hf)
                own_sel[hf].start()
            for way in range(2):
                if used(way, step, hf):
                    if step > 0:
                        ring(way, step - 1, hf).wait_recv()
                    ring(way, step, hf).start()
        if step == steps // 2:
            across.wait_recv()
            onward = column(2, cols.at[x_peer], x_peer, core_peer)
            onward.start()

    for way in range(2):
        for step in range(steps):
            for hf in range(2):
                if used(way, step, hf):
                    if step == steps - 1 or not used(way, step + 1, hf):
                        ring(way, step, hf).wait_recv()
    beside.wait_recv()
    onward.wait_recv()
    for copy in meta_copies:
        copy.wait_recv()

    each_scatter(0, lambda copy: copy.wait_send())
    each_scatter(1, lambda copy: copy.wait_send())
    across.wait_send()
    beside.wait_send()
    onward.wait_send()
    for copy in meta_copies:
        copy.wait_send()
    for way in range(2):
        for step in range(steps):
            for hf in range(2):
                if used(way, step, hf):
                    ring(way, step, hf).wait_send()
    own_col.wait()
    own_meta.wait()
    for copy in own_sel:
        copy.wait()


def tiles_kernel(nt, group, no, metas, plan, occ, gt, cols, virt, out, acc, base):
    j = pl.program_id(0)
    ng = out.shape[0]
    qa = gt.shape[1]
    steps = nt // ng
    g = lax.axis_index("grp")
    o = lax.axis_index("orb")

    @pl.when(j == 0)
    def _():
        acc[...] = jnp.zeros_like(acc)
        rows = jnp.broadcast_to(virt[:, pl.ds(pl.multiple_of(g * qa, 128), qa)], (qa, qa)).T
        for k in range(out.shape[2] // qa):
            at = slice(k * qa, (k + 1) * qa)
            base[:, at] = rows + virt[:, at]

    own = occ[j * no + o]
    right = cols[0]
    for first in range(0, nt, group):
        left = gt[first : first + group].reshape(group * qa, gt.shape[2])
        integral = jnp.dot(left, right, preferred_element_type=jnp.float32)
        for k in range(group):
            hf, rest = divmod(first + k, nt // 2)
            c, s = divmod(rest, steps)
            h = lax.rem(g // 2 + hf, 2) * 2 + c
            t = s * ng + h
            weight = metas[j, 0, t]
            owner = metas[j, 1, t].astype(jnp.int32)
            denominator = base[...] - occ[h * no + plan[s, h]] - own
            amplitude = integral[k * qa : (k + 1) * qa] / denominator * weight
            acc[owner] = acc[owner] + amplitude.astype(jnp.bfloat16).astype(jnp.float32)

    @pl.when(j == ng - 1)
    def _():
        out[...] = acc[...].astype(out.dtype)


def split_kernel(virt, off, high, low):
    n = off.shape[0]
    rows = lax.broadcasted_iota(jnp.int32, (n, n), 0)
    columns = lax.broadcasted_iota(jnp.int32, (n, n), 1)
    fock = jnp.where(rows == columns, virt[...], 0.0) + 0.5 * (off[...] + off[...].T)
    top = fock.astype(jnp.bfloat16)
    high[...] = top
    low[...] = (fock - top.astype(jnp.float32)).astype(jnp.bfloat16)


def fock_kernel(summed, high, low, out):
    s = summed[...]
    h = high[...]
    l = low[...]
    dot = functools.partial(jnp.dot, preferred_element_type=jnp.float32)
    out[...] = (dot(h, s) + dot(s, h)) + (dot(l, s) + dot(s, l))


def shards(df_panels, occ_energy, virt_energy, fock_off, i_plan, pair_owner, pair_weight):
    ng = lax.axis_size("grp")
    no = lax.axis_size("orb")
    panel = df_panels[0]
    naux, nvir = panel.shape
    nt = pair_owner.shape[0]
    qa = nvir // ng
    f32 = jnp.float32
    vmem = pl.BlockSpec(memory_space=pltpu.VMEM)
    smem = pl.BlockSpec(memory_space=pltpu.SMEM)
    hbm = pl.BlockSpec(memory_space=pl.ANY)
    dma = pltpu.SemaphoreType.DMA

    nc = no // ROWS
    gt, cols, metas = pl.pallas_call(
        functools.partial(gather_kernel, ng, no, nt),
        out_shape=[
            jax.ShapeDtypeStruct((nt, qa, naux), jnp.bfloat16),
            jax.ShapeDtypeStruct((ng, naux, nvir), jnp.bfloat16),
            jax.ShapeDtypeStruct((ng, 8, 128), f32),
        ],
        in_specs=[smem, vmem, vmem, hbm, hbm],
        out_specs=[hbm, hbm, hbm],
        scratch_shapes=[
            pltpu.VMEM((8, 128), f32),
            pltpu.VMEM((2 * no, qa // ROWS, naux // nc), jnp.bfloat16),
            pltpu.VMEM((2 * no, qa // ROWS, naux // nc), jnp.bfloat16),
            pltpu.VMEM((nt, qa // ROWS, naux // nc), jnp.bfloat16),
            dma((2, 2 * no)),
            dma((2, 2 * no)),
            dma((3,)),
            dma((3,)),
            dma((3,)),
            dma((3,)),
            dma((2, no // 2, 2)),
            dma((2, no // 2, 2)),
            dma((5,)),
        ],
        compiler_params=pltpu.CompilerParams(has_side_effects=True),
        name="gather_panels",
    )(i_plan, pair_weight.reshape(1, nt), pair_owner.reshape(1, nt), panel.T, panel)

    virt_row = virt_energy[None, :]
    group = 4
    parts = pl.pallas_call(
        functools.partial(tiles_kernel, nt, group, no),
        grid=(ng,),
        out_shape=jax.ShapeDtypeStruct((ng, qa, nvir), jnp.bfloat16),
        in_specs=[
            smem,
            smem,
            smem,
            vmem,
            pl.BlockSpec((1, naux, nvir), lambda j: (j, 0, 0)),
            vmem,
        ],
        out_specs=vmem,
        scratch_shapes=[pltpu.VMEM((ng, qa, nvir), f32), pltpu.VMEM((qa, nvir), f32)],
        compiler_params=pltpu.CompilerParams(vmem_limit_bytes=60 * 2**20),
        name="pair_tiles",
    )(metas, i_plan, occ_energy, gt, cols, virt_row)

    summed = lax.all_to_all(parts, "grp", split_axis=0, concat_axis=0, tiled=True)
    summed = summed.reshape(nvir, nvir)
    high, low = pl.pallas_call(
        split_kernel,
        out_shape=[jax.ShapeDtypeStruct((nvir, nvir), jnp.bfloat16)] * 2,
        in_specs=[vmem] * 2,
        out_specs=[vmem] * 2,
        cost_estimate=pl.CostEstimate(flops=4 * nvir * nvir, bytes_accessed=8 * nvir * nvir, transcendentals=0),
        name="fock_split",
    )(virt_row, fock_off)
    residual = pl.pallas_call(
        fock_kernel,
        out_shape=jax.ShapeDtypeStruct((nvir, nvir), f32),
        in_specs=[vmem] * 3,
        out_specs=vmem,
        compiler_params=pltpu.CompilerParams(vmem_limit_bytes=60 * 2**20),
        name="fock_products",
    )(summed, high, low)
    return residual[None]


def solution(mesh):
    placed = (
        P(("grp", "orb"), None, None),
        P(),
        P(),
        P(),
        P(),
        P(("grp", "orb"), None),
        P(("grp", "orb")),
    )
    return jax.shard_map(
        shards, mesh=mesh, in_specs=placed, out_specs=P(("grp", "orb"), None, None), check_vma=False
    )
```

```python
import functools

import jax
import jax.numpy as jnp
from jax import lax
from jax.experimental import pallas as pl
from jax.experimental.pallas import tpu as pltpu
from jax.sharding import PartitionSpec as P

MESH = pl.DeviceIdType.MESH
ROWS = 8


def ring_orb(pos, n):
    half = n // 2
    return jnp.where(pos < half, 2 * pos, 2 * (n - 1 - pos) + 1)


def gather_kernel(
    ng, no, nt, plan, weight, owner, panel_t, panel, gt, cols, metas,
    meta, pieces_here, pieces_over, sel, sc_send, sc_recv, col_send, col_recv, meta_send, meta_recv,
    ring_send, ring_recv, loc,
):
    g = lax.axis_index("grp")
    o = lax.axis_index("orb")
    nvir, naux = panel_t.shape
    qa = nvir // ng
    ra = qa // ROWS
    nc = no // ROWS
    wa = naux // nc
    half_t = nt // 2

    def piece_of(orb):
        return orb // nc, orb % nc

    def block_in_panel(q, orb):
        r, c = piece_of(orb)
        return panel_t.at[
            pl.ds(pl.multiple_of(q * qa + r * ra, 16), ra), pl.ds(pl.multiple_of(c * wa, 128), wa)
        ]

    pieces = (pieces_here, pieces_over)
    gx, gc = g // 2, lax.rem(g, 2)
    side = 2 * no
    place = gc * no + o

    def scatter(hf, k):
        to = lax.rem(gx + hf, 2) * side + lax.rem(place + k, side)
        q, orb = to // no, lax.rem(to, no)
        return pltpu.make_async_remote_copy(
            src_ref=block_in_panel(q, orb),
            dst_ref=pieces[hf].at[place],
            send_sem=sc_send.at[hf, k],
            recv_sem=sc_recv.at[hf, k],
            device_id=(q, orb),
            device_id_type=MESH,
        )

    own_piece = pltpu.make_async_copy(block_in_panel(g, o), pieces_here.at[place], loc.at[0])
    own_piece.start()

    def each_scatter(hf, act):
        def body(k, carry):
            act(scatter(hf, k))
            return carry

        lax.fori_loop(1 - hf, side, body, 0)

    each_scatter(0, lambda copy: copy.start())
    each_scatter(1, lambda copy: copy.start())
    meta[...] = jnp.zeros_like(meta)
    meta[0:1, 0:nt] = weight[...]
    meta[1:2, 0:nt] = owner[...].astype(jnp.float32)

    core_peer = gx * 2 + 1 - gc
    x_peer = (1 - gx) * 2 + gc
    diag_peer = (1 - gx) * 2 + 1 - gc

    def column(index, src, slot, to):
        return pltpu.make_async_remote_copy(
            src_ref=src,
            dst_ref=cols.at[slot],
            send_sem=col_send.at[index],
            recv_sem=col_recv.at[index],
            device_id=(to, o),
            device_id_type=MESH,
        )

    across = column(0, panel, g, x_peer)
    beside = column(1, panel, g, core_peer)
    across.start()
    beside.start()
    own_col = pltpu.make_async_copy(panel, cols.at[g], loc.at[1])
    own_col.start()
    own_meta = pltpu.make_async_copy(meta, metas.at[g], loc.at[2])
    own_meta.start()
    meta_copies = []
    for index, to in enumerate((core_peer, x_peer, diag_peer)):
        copy = pltpu.make_async_remote_copy(
            src_ref=meta,
            dst_ref=metas.at[g],
            send_sem=meta_send.at[index],
            recv_sem=meta_recv.at[index],
            device_id=(to, o),
            device_id_type=MESH,
        )
        copy.start()
        meta_copies.append(copy)

    own_piece.wait()

    def select(hf):
        side_x = lax.rem(gx + hf, 2)
        for c in range(2):
            for s in range(nt // ng):
                h = side_x * 2 + c
                sel[hf * half_t + c * (nt // ng) + s] = pieces[hf][c * no + plan[s, h]]

    def block_in_gt(hf, orb):
        r, c = piece_of(orb)
        return gt.at[
            pl.ds(hf * half_t, half_t),
            pl.ds(pl.multiple_of(r * ra, 16), ra),
            pl.ds(pl.multiple_of(c * wa, 128), wa),
        ]

    own_sel = [
        pltpu.make_async_copy(
            sel.at[pl.ds(hf * half_t, half_t)], block_in_gt(hf, o), loc.at[3 + hf]
        )
        for hf in range(2)
    ]

    pos = jnp.where(lax.rem(o, 2) == 0, o // 2, no - 1 - o // 2)
    steps = no // 2
    next_orb = (
        ring_orb(lax.rem(pos + 1, no), no),
        ring_orb(lax.rem(pos + no - 1, no), no),
    )

    def ring(way, step, hf):
        origin = lax.rem(pos + (no - step if way == 0 else step), no)
        orb = ring_orb(origin, no)
        src = block_in_gt(hf, orb)
        if step == 0:
            src = sel.at[pl.ds(hf * half_t, half_t)]
        return pltpu.make_async_remote_copy(
            src_ref=src,
            dst_ref=block_in_gt(hf, orb),
            send_sem=ring_send.at[way, step, hf],
            recv_sem=ring_recv.at[way, step, hf],
            device_id=(g, next_orb[way]),
            device_id_type=MESH,
        )

    def used(way, step, hf):
        return step < steps - 1 or hf == way

    for step in range(steps):
        for hf in range(2):
            if step == 0:
                each_scatter(hf, lambda copy: copy.wait_recv())
                select(hf)
                own_sel[hf].start()
            for way in range(2):
                if used(way, step, hf):
                    if step > 0:
                        ring(way, step - 1, hf).wait_recv()
                    ring(way, step, hf).start()
        if step == steps - 1:
            across.wait_recv()
            onward = column(2, cols.at[x_peer], x_peer, core_peer)
            onward.start()

    for way in range(2):
        for step in range(steps):
            for hf in range(2):
                if used(way, step, hf):
                    if step == steps - 1 or not used(way, step + 1, hf):
                        ring(way, step, hf).wait_recv()
    beside.wait_recv()
    onward.wait_recv()
    for copy in meta_copies:
        copy.wait_recv()

    each_scatter(0, lambda copy: copy.wait_send())
    each_scatter(1, lambda copy: copy.wait_send())
    across.wait_send()
    beside.wait_send()
    onward.wait_send()
    for copy in meta_copies:
        copy.wait_send()
    for way in range(2):
        for step in range(steps):
            for hf in range(2):
                if used(way, step, hf):
                    ring(way, step, hf).wait_send()
    own_col.wait()
    own_meta.wait()
    for copy in own_sel:
        copy.wait()


def tiles_kernel(nt, group, no, metas, plan, occ, gt, cols, virt, out, acc, base):
    j = pl.program_id(0)
    ng = out.shape[0]
    qa = gt.shape[1]
    steps = nt // ng
    g = lax.axis_index("grp")
    o = lax.axis_index("orb")

    @pl.when(j == 0)
    def _():
        acc[...] = jnp.zeros_like(acc)
        rows = jnp.broadcast_to(virt[:, pl.ds(pl.multiple_of(g * qa, 128), qa)], (qa, qa)).T
        for k in range(out.shape[2] // qa):
            at = slice(k * qa, (k + 1) * qa)
            base[:, at] = rows + virt[:, at]

    own = occ[j * no + o]
    right = cols[0]
    for first in range(0, nt, group):
        left = gt[first : first + group].reshape(group * qa, gt.shape[2])
        integral = jnp.dot(left, right, preferred_element_type=jnp.float32)
        for k in range(group):
            hf, rest = divmod(first + k, nt // 2)
            c, s = divmod(rest, steps)
            h = lax.rem(g // 2 + hf, 2) * 2 + c
            t = s * ng + h
            weight = metas[j, 0, t]
            owner = metas[j, 1, t].astype(jnp.int32)
            denominator = base[...] - occ[h * no + plan[s, h]] - own
            amplitude = integral[k * qa : (k + 1) * qa] / denominator * weight
            acc[owner] = acc[owner] + amplitude.astype(jnp.bfloat16).astype(jnp.float32)

    @pl.when(j == ng - 1)
    def _():
        out[...] = acc[...].astype(out.dtype)


def split_kernel(virt, off, high, low):
    n = off.shape[0]
    rows = lax.broadcasted_iota(jnp.int32, (n, n), 0)
    columns = lax.broadcasted_iota(jnp.int32, (n, n), 1)
    fock = jnp.where(rows == columns, virt[...], 0.0) + 0.5 * (off[...] + off[...].T)
    top = fock.astype(jnp.bfloat16)
    high[...] = top
    low[...] = (fock - top.astype(jnp.float32)).astype(jnp.bfloat16)


def fock_kernel(summed, high, low, out):
    s = summed[...]
    h = high[...]
    l = low[...]
    dot = functools.partial(jnp.dot, preferred_element_type=jnp.float32)
    out[...] = (dot(h, s) + dot(s, h)) + (dot(l, s) + dot(s, l))


def shards(df_panels, occ_energy, virt_energy, fock_off, i_plan, pair_owner, pair_weight):
    ng = lax.axis_size("grp")
    no = lax.axis_size("orb")
    panel = df_panels[0]
    naux, nvir = panel.shape
    nt = pair_owner.shape[0]
    qa = nvir // ng
    f32 = jnp.float32
    vmem = pl.BlockSpec(memory_space=pltpu.VMEM)
    smem = pl.BlockSpec(memory_space=pltpu.SMEM)
    hbm = pl.BlockSpec(memory_space=pl.ANY)
    dma = pltpu.SemaphoreType.DMA

    nc = no // ROWS
    gt, cols, metas = pl.pallas_call(
        functools.partial(gather_kernel, ng, no, nt),
        out_shape=[
            jax.ShapeDtypeStruct((nt, qa, naux), jnp.bfloat16),
            jax.ShapeDtypeStruct((ng, naux, nvir), jnp.bfloat16),
            jax.ShapeDtypeStruct((ng, 8, 128), f32),
        ],
        in_specs=[smem, vmem, vmem, hbm, hbm],
        out_specs=[hbm, hbm, hbm],
        scratch_shapes=[
            pltpu.VMEM((8, 128), f32),
            pltpu.VMEM((2 * no, qa // ROWS, naux // nc), jnp.bfloat16),
            pltpu.VMEM((2 * no, qa // ROWS, naux // nc), jnp.bfloat16),
            pltpu.VMEM((nt, qa // ROWS, naux // nc), jnp.bfloat16),
            dma((2, 2 * no)),
            dma((2, 2 * no)),
            dma((3,)),
            dma((3,)),
            dma((3,)),
            dma((3,)),
            dma((2, no // 2, 2)),
            dma((2, no // 2, 2)),
            dma((5,)),
        ],
        compiler_params=pltpu.CompilerParams(has_side_effects=True),
        name="gather_panels",
    )(i_plan, pair_weight.reshape(1, nt), pair_owner.reshape(1, nt), panel.T, panel)

    virt_row = virt_energy[None, :]
    group = 4
    parts = pl.pallas_call(
        functools.partial(tiles_kernel, nt, group, no),
        grid=(ng,),
        out_shape=jax.ShapeDtypeStruct((ng, qa, nvir), jnp.bfloat16),
        in_specs=[
            smem,
            smem,
            smem,
            vmem,
            pl.BlockSpec((1, naux, nvir), lambda j: (j, 0, 0)),
            vmem,
        ],
        out_specs=vmem,
        scratch_shapes=[pltpu.VMEM((ng, qa, nvir), f32), pltpu.VMEM((qa, nvir), f32)],
        compiler_params=pltpu.CompilerParams(vmem_limit_bytes=60 * 2**20),
        name="pair_tiles",
    )(metas, i_plan, occ_energy, gt, cols, virt_row)

    summed = lax.all_to_all(parts, "grp", split_axis=0, concat_axis=0, tiled=True)
    summed = summed.reshape(nvir, nvir)
    high, low = pl.pallas_call(
        split_kernel,
        out_shape=[jax.ShapeDtypeStruct((nvir, nvir), jnp.bfloat16)] * 2,
        in_specs=[vmem] * 2,
        out_specs=[vmem] * 2,
        cost_estimate=pl.CostEstimate(flops=4 * nvir * nvir, bytes_accessed=8 * nvir * nvir, transcendentals=0),
        name="fock_split",
    )(virt_row, fock_off)
    residual = pl.pallas_call(
        fock_kernel,
        out_shape=jax.ShapeDtypeStruct((nvir, nvir), f32),
        in_specs=[vmem] * 3,
        out_specs=vmem,
        compiler_params=pltpu.CompilerParams(vmem_limit_bytes=60 * 2**20),
        name="fock_products",
    )(summed, high, low)
    return residual[None]


def solution(mesh):
    placed = (
        P(("grp", "orb"), None, None),
        P(),
        P(),
        P(),
        P(),
        P(("grp", "orb"), None),
        P(("grp", "orb")),
    )
    return jax.shard_map(
        shards, mesh=mesh, in_specs=placed, out_specs=P(("grp", "orb"), None, None), check_vma=False
    )
```

```python
import functools

import jax
import jax.numpy as jnp
from jax import lax
from jax.experimental import pallas as pl
from jax.experimental.pallas import tpu as pltpu
from jax.sharding import PartitionSpec as P

MESH = pl.DeviceIdType.MESH
ROWS = 8


def ring_orb(pos, n):
    half = n // 2
    return jnp.where(pos < half, 2 * pos, 2 * (n - 1 - pos) + 1)


def gather_kernel(
    ng, no, nt, plan, weight, owner, panel_t, panel, gt, cols, metas,
    meta, pieces_here, pieces_over, sel, sc_send, sc_recv, col_send, col_recv, meta_send, meta_recv,
    ring_send, ring_recv, loc,
):
    g = lax.axis_index("grp")
    o = lax.axis_index("orb")
    nvir, naux = panel_t.shape
    qa = nvir // ng
    ra = qa // ROWS
    nc = no // ROWS
    wa = naux // nc
    half_t = nt // 2

    def piece_of(orb):
        return orb // nc, orb % nc

    def block_in_panel(q, orb):
        r, c = piece_of(orb)
        return panel_t.at[
            pl.ds(pl.multiple_of(q * qa + r * ra, 16), ra), pl.ds(pl.multiple_of(c * wa, 128), wa)
        ]

    pieces = (pieces_here, pieces_over)
    gx, gc = g // 2, lax.rem(g, 2)
    side = 2 * no
    place = gc * no + o

    def scatter(hf, k):
        to = lax.rem(gx + hf, 2) * side + lax.rem(place + k, side)
        q, orb = to // no, lax.rem(to, no)
        return pltpu.make_async_remote_copy(
            src_ref=block_in_panel(q, orb),
            dst_ref=pieces[hf].at[place],
            send_sem=sc_send.at[hf, k],
            recv_sem=sc_recv.at[hf, k],
            device_id=(q, orb),
            device_id_type=MESH,
        )

    own_piece = pltpu.make_async_copy(block_in_panel(g, o), pieces_here.at[place], loc.at[0])
    own_piece.start()

    def each_scatter(hf, act):
        def body(k, carry):
            act(scatter(hf, k))
            return carry

        lax.fori_loop(1 - hf, side, body, 0)

    each_scatter(0, lambda copy: copy.start())
    each_scatter(1, lambda copy: copy.start())
    meta[...] = jnp.zeros_like(meta)
    meta[0:1, 0:nt] = weight[...]
    meta[1:2, 0:nt] = owner[...].astype(jnp.float32)

    core_peer = gx * 2 + 1 - gc
    x_peer = (1 - gx) * 2 + gc
    diag_peer = (1 - gx) * 2 + 1 - gc

    def column(index, src, slot, to):
        return pltpu.make_async_remote_copy(
            src_ref=src,
            dst_ref=cols.at[slot],
            send_sem=col_send.at[index],
            recv_sem=col_recv.at[index],
            device_id=(to, o),
            device_id_type=MESH,
        )

    across = column(0, panel, g, x_peer)
    beside = column(1, panel, g, core_peer)
    across.start()
    beside.start()
    own_col = pltpu.make_async_copy(panel, cols.at[g], loc.at[1])
    own_col.start()
    own_meta = pltpu.make_async_copy(meta, metas.at[g], loc.at[2])
    own_meta.start()
    meta_copies = []
    for index, to in enumerate((core_peer, x_peer, diag_peer)):
        copy = pltpu.make_async_remote_copy(
            src_ref=meta,
            dst_ref=metas.at[g],
            send_sem=meta_send.at[index],
            recv_sem=meta_recv.at[index],
            device_id=(to, o),
            device_id_type=MESH,
        )
        copy.start()
        meta_copies.append(copy)

    own_piece.wait()

    def select(hf):
        side_x = lax.rem(gx + hf, 2)
        for c in range(2):
            for s in range(nt // ng):
                h = side_x * 2 + c
                sel[hf * half_t + c * (nt // ng) + s] = pieces[hf][c * no + plan[s, h]]

    def block_in_gt(hf, orb):
        r, c = piece_of(orb)
        return gt.at[
            pl.ds(hf * half_t, half_t),
            pl.ds(pl.multiple_of(r * ra, 16), ra),
            pl.ds(pl.multiple_of(c * wa, 128), wa),
        ]

    own_sel = [
        pltpu.make_async_copy(
            sel.at[pl.ds(hf * half_t, half_t)], block_in_gt(hf, o), loc.at[3 + hf]
        )
        for hf in range(2)
    ]

    pos = jnp.where(lax.rem(o, 2) == 0, o // 2, no - 1 - o // 2)
    steps = no // 2
    next_orb = (
        ring_orb(lax.rem(pos + 1, no), no),
        ring_orb(lax.rem(pos + no - 1, no), no),
    )

    def ring(way, step, hf):
        origin = lax.rem(pos + (no - step if way == 0 else step), no)
        orb = ring_orb(origin, no)
        src = block_in_gt(hf, orb)
        if step == 0:
            src = sel.at[pl.ds(hf * half_t, half_t)]
        return pltpu.make_async_remote_copy(
            src_ref=src,
            dst_ref=block_in_gt(hf, orb),
            send_sem=ring_send.at[way, step, hf],
            recv_sem=ring_recv.at[way, step, hf],
            device_id=(g, next_orb[way]),
            device_id_type=MESH,
        )

    def used(way, step, hf):
        return step < steps - 1 or hf == way

    for step in range(steps):
        for hf in range(2):
            if step == 0:
                each_scatter(hf, lambda copy: copy.wait_recv())
                select(hf)
                own_sel[hf].start()
            for way in range(2):
                if used(way, step, hf):
                    if step > 0:
                        ring(way, step - 1, hf).wait_recv()
                    ring(way, step, hf).start()
        if step == steps // 2:
            across.wait_recv()
            onward = column(2, cols.at[x_peer], x_peer, core_peer)
            onward.start()

    for way in range(2):
        for step in range(steps):
            for hf in range(2):
                if used(way, step, hf):
                    if step == steps - 1 or not used(way, step + 1, hf):
                        ring(way, step, hf).wait_recv()
    beside.wait_recv()
    onward.wait_recv()
    for copy in meta_copies:
        copy.wait_recv()

    each_scatter(0, lambda copy: copy.wait_send())
    each_scatter(1, lambda copy: copy.wait_send())
    across.wait_send()
    beside.wait_send()
    onward.wait_send()
    for copy in meta_copies:
        copy.wait_send()
    for way in range(2):
        for step in range(steps):
            for hf in range(2):
                if used(way, step, hf):
                    ring(way, step, hf).wait_send()
    own_col.wait()
    own_meta.wait()
    for copy in own_sel:
        copy.wait()


def tiles_kernel(nt, group, no, metas, plan, occ, gt, cols, virt, out, acc, base):
    j = pl.program_id(0)
    ng = out.shape[0]
    qa = gt.shape[1]
    steps = nt // ng
    g = lax.axis_index("grp")
    o = lax.axis_index("orb")

    @pl.when(j == 0)
    def _():
        acc[...] = jnp.zeros_like(acc)
        rows = jnp.broadcast_to(virt[:, pl.ds(pl.multiple_of(g * qa, 128), qa)], (qa, qa)).T
        for k in range(out.shape[2] // qa):
            at = slice(k * qa, (k + 1) * qa)
            base[:, at] = rows + virt[:, at]

    own = occ[j * no + o]
    right = cols[0]
    for first in range(0, nt, group):
        left = gt[first : first + group].reshape(group * qa, gt.shape[2])
        integral = jnp.dot(left, right, preferred_element_type=jnp.float32)
        for k in range(group):
            hf, rest = divmod(first + k, nt // 2)
            c, s = divmod(rest, steps)
            h = lax.rem(g // 2 + hf, 2) * 2 + c
            t = s * ng + h
            weight = metas[j, 0, t]
            owner = metas[j, 1, t].astype(jnp.int32)
            denominator = base[...] - occ[h * no + plan[s, h]] - own
            amplitude = integral[k * qa : (k + 1) * qa] / denominator * weight
            acc[owner] = acc[owner] + amplitude.astype(jnp.bfloat16).astype(jnp.float32)

    @pl.when(j == ng - 1)
    def _():
        out[...] = acc[...].astype(out.dtype)


def exchange_kernel(ng, parts, virt, off, summed, high, low, send, recv, loc):
    g = lax.axis_index("grp")
    o = lax.axis_index("orb")
    copies = []
    for k in range(ng - 1, 0, -1):
        to = lax.rem(g + k, ng)
        copy = pltpu.make_async_remote_copy(
            src_ref=parts.at[to],
            dst_ref=summed.at[g],
            send_sem=send.at[k],
            recv_sem=recv.at[k],
            device_id=(to, o),
            device_id_type=MESH,
        )
        copy.start()
        copies.append(copy)
    own = pltpu.make_async_copy(parts.at[g], summed.at[g], loc.at[0])
    own.start()
    n = off.shape[0]
    rows = lax.broadcasted_iota(jnp.int32, (n, n), 0)
    columns = lax.broadcasted_iota(jnp.int32, (n, n), 1)
    fock = jnp.where(rows == columns, virt[...], 0.0) + 0.5 * (off[...] + off[...].T)
    top = fock.astype(jnp.bfloat16)
    high[...] = top
    low[...] = (fock - top.astype(jnp.float32)).astype(jnp.bfloat16)
    own.wait()
    for copy in copies:
        copy.wait()


def fock_kernel(summed, high, low, out):
    s = summed[...]
    h = high[...]
    l = low[...]
    dot = functools.partial(jnp.dot, preferred_element_type=jnp.float32)
    out[...] = (dot(h, s) + dot(s, h)) + (dot(l, s) + dot(s, l))


def shards(df_panels, occ_energy, virt_energy, fock_off, i_plan, pair_owner, pair_weight):
    ng = lax.axis_size("grp")
    no = lax.axis_size("orb")
    panel = df_panels[0]
    naux, nvir = panel.shape
    nt = pair_owner.shape[0]
    qa = nvir // ng
    f32 = jnp.float32
    vmem = pl.BlockSpec(memory_space=pltpu.VMEM)
    smem = pl.BlockSpec(memory_space=pltpu.SMEM)
    hbm = pl.BlockSpec(memory_space=pl.ANY)
    dma = pltpu.SemaphoreType.DMA

    nc = no // ROWS
    gt, cols, metas = pl.pallas_call(
        functools.partial(gather_kernel, ng, no, nt),
        out_shape=[
            jax.ShapeDtypeStruct((nt, qa, naux), jnp.bfloat16),
            jax.ShapeDtypeStruct((ng, naux, nvir), jnp.bfloat16),
            jax.ShapeDtypeStruct((ng, 8, 128), f32),
        ],
        in_specs=[smem, vmem, vmem, hbm, hbm],
        out_specs=[hbm, hbm, hbm],
        scratch_shapes=[
            pltpu.VMEM((8, 128), f32),
            pltpu.VMEM((2 * no, qa // ROWS, naux // nc), jnp.bfloat16),
            pltpu.VMEM((2 * no, qa // ROWS, naux // nc), jnp.bfloat16),
            pltpu.VMEM((nt, qa // ROWS, naux // nc), jnp.bfloat16),
            dma((2, 2 * no)),
            dma((2, 2 * no)),
            dma((3,)),
            dma((3,)),
            dma((3,)),
            dma((3,)),
            dma((2, no // 2, 2)),
            dma((2, no // 2, 2)),
            dma((5,)),
        ],
        compiler_params=pltpu.CompilerParams(has_side_effects=True),
        name="gather_panels",
    )(i_plan, pair_weight.reshape(1, nt), pair_owner.reshape(1, nt), panel.T, panel)

    virt_row = virt_energy[None, :]
    group = 4
    parts = pl.pallas_call(
        functools.partial(tiles_kernel, nt, group, no),
        grid=(ng,),
        out_shape=jax.ShapeDtypeStruct((ng, qa, nvir), jnp.bfloat16),
        in_specs=[
            smem,
            smem,
            smem,
            vmem,
            pl.BlockSpec((1, naux, nvir), lambda j: (j, 0, 0)),
            vmem,
        ],
        out_specs=vmem,
        scratch_shapes=[pltpu.VMEM((ng, qa, nvir), f32), pltpu.VMEM((qa, nvir), f32)],
        compiler_params=pltpu.CompilerParams(vmem_limit_bytes=60 * 2**20),
        name="pair_tiles",
    )(metas, i_plan, occ_energy, gt, cols, virt_row)

    summed, high, low = pl.pallas_call(
        functools.partial(exchange_kernel, ng),
        out_shape=[jax.ShapeDtypeStruct((ng, qa, nvir), jnp.bfloat16)]
        + [jax.ShapeDtypeStruct((nvir, nvir), jnp.bfloat16)] * 2,
        in_specs=[hbm, vmem, vmem],
        out_specs=[hbm, vmem, vmem],
        scratch_shapes=[dma((ng,)), dma((ng,)), dma((1,))],
        compiler_params=pltpu.CompilerParams(has_side_effects=True),
        name="exchange_sums",
    )(parts, virt_row, fock_off)
    summed = summed.reshape(nvir, nvir)
    residual = pl.pallas_call(
        fock_kernel,
        out_shape=jax.ShapeDtypeStruct((nvir, nvir), f32),
        in_specs=[vmem] * 3,
        out_specs=vmem,
        compiler_params=pltpu.CompilerParams(vmem_limit_bytes=60 * 2**20),
        name="fock_products",
    )(summed, high, low)
    return residual[None]


def solution(mesh):
    placed = (
        P(("grp", "orb"), None, None),
        P(),
        P(),
        P(),
        P(),
        P(("grp", "orb"), None),
        P(("grp", "orb")),
    )
    return jax.shard_map(
        shards, mesh=mesh, in_specs=placed, out_specs=P(("grp", "orb"), None, None), check_vma=False
    )
```
